32 devices in a mesh: groups: 2 (over y), pair: 4 (over z), ints: 2 (over x), rep: 2 (over core).
Axes of the slice: x: 2, y: 2, z: 4, core: 2. Of those that a mesh axis runs over, the one named last changes fastest.
Arguments:
- amplitudes: bfloat16 [1024, 16, 4096], P(('groups', 'pair', 'ints', 'rep')), parts along dimension 0, may hold values from -6 to 6
- integrals: bfloat16 [256, 65536], P(('groups', 'ints'), 'pair'), parts along dimension 0, may hold values from -0.03125 to 0.03125
- pair_irrep: int32 [1024], P(('groups', 'pair', 'ints', 'rep')), parts along dimension 0, may hold values from 0 to 1
- slot_irrep: int32 [32], P('groups'), parts along dimension 0, may hold values from 0 to 1, as said below
- owner_slot_map: int32 [32], P('groups'), parts along dimension 0, may hold values from 0 to 15, each once
Outputs:
- ladder: float32 [1024, 128], P(('groups', 'pair', 'ints', 'rep')), parts along dimension 0
The draws below stay inside these ranges and needn't reach their ends.
There are 2 independent parts, one for each index of `groups`. The reference program is written for one: setup_inputs(seed, part) draws one part's arguments, and reference() takes and returns one part's arrays. A program takes and returns all parts, laid end to end along the dimension named above; each array names one. Nothing has to cross between parts.
Inputs may be any that keep to these rules, and one draw needn't show every extreme that they name: `slot_irrep`: every irrep labels the same number of slots.
All inputs are finite; a program needn't handle non-finite values.
Results may differ from the reference program's by a relative error of at most 0.0003.
Values may be sent and summed in bfloat16 or wider, within the bound.
No kernel may reach another device: no remote copies, remote signals or barrier semaphores. Data moves between devices by JAX's collectives and lax.ppermute only.
A program may use at most 64 MiB of HBM per device.

```python
import jax
import jax.numpy as jnp

TILE_ORBITALS = 64
STORED_SLOTS = 16
IRREPS = 2
OCCUPIED_PAIRS = 512
AB = 128
CD = 65536


def draw_slot_irrep(key, part):
    key = jax.random.fold_in(key, 7)
    owner_ordering = jax.random.permutation(key, STORED_SLOTS)
    return (owner_ordering % IRREPS).astype(jnp.int32)


def with_ends(result, stream_key, smallest, largest):
    longest = result.shape.index(max(result.shape))
    spots = []
    for shift in (0, 1):
        where = [jax.random.randint(jax.random.fold_in(stream_key, axis), (), 0, length) for axis, length in enumerate(result.shape)]
        where[longest] = (where[longest] + shift) % result.shape[longest]
        spots.append(tuple(where))
    return result.at[spots[0]].set(smallest).at[spots[1]].set(largest)


def level_of(key, shape, split, smallest, top_value):
    loudness = 1.0
    for dim, shards_of in split:
        steps = jax.random.uniform(jax.random.fold_in(jax.random.fold_in(key, 6), dim), (shards_of,), jnp.float32, smallest / len(split), top_value / len(split))
        loudness = loudness * jnp.repeat(jnp.exp(steps), shape[dim] // shards_of).reshape((-1,) + (1,) * (len(shape) - 1 - dim))
    return loudness


def centred(own_key, extent, spread, bound, pieces=(), held_as=jnp.bfloat16):
    loudness = level_of(own_key, extent, pieces, -0.22, 0.18) if pieces else 1.0
    array = jax.random.normal(own_key, extent, jnp.float32) * spread * loudness
    return jnp.minimum(jnp.maximum(array, -bound), bound).astype(held_as)


def setup_inputs(seed: int = 0, part: int = 0) -> dict:
    key_of = jax.random.split(jax.random.key(seed), 6)
    own_keys = jax.random.split(jax.random.fold_in(key_of[5], part), 6)
    return {
        "amplitudes": centred(own_keys[0], (OCCUPIED_PAIRS, STORED_SLOTS, TILE_ORBITALS * TILE_ORBITALS), 1.0, 6.0, ((0, 16),)),
        "integrals": centred(own_keys[1], (AB, CD), (CD // IRREPS) ** -0.5, 0.03125, ((0, 2), (1, 4))),
        "pair_irrep": with_ends(jax.random.randint(own_keys[2], (OCCUPIED_PAIRS,), 0, IRREPS), jax.random.fold_in(own_keys[2], 1), 0, IRREPS - 1).astype(jnp.int32),
        "slot_irrep": draw_slot_irrep(jax.random.fold_in(jax.random.fold_in(key_of[5], part), 71), part),
        "owner_slot_map": jax.random.permutation(own_keys[4], STORED_SLOTS).astype(jnp.int32),
    }


def reference(amplitudes, integrals, pair_irrep, slot_irrep, owner_slot_map):
    slot_position_index = jnp.arange(STORED_SLOTS, dtype=jnp.int32)
    choose = owner_slot_map[:, None] == slot_position_index[None, :]
    owner_irrep = jnp.sum(jnp.where(choose, slot_irrep[None, :], 0), axis=1).astype(jnp.int32)
    sorted_slots = jnp.take(amplitudes, owner_slot_map, axis=1)
    live_tiles = pair_irrep[:, None] == owner_irrep[None, :]
    sorted_slots = jnp.where(live_tiles[:, :, None], sorted_slots, jnp.zeros((), amplitudes.dtype))
    sorted_slots = sorted_slots.reshape(OCCUPIED_PAIRS, STORED_SLOTS * TILE_ORBITALS * TILE_ORBITALS)
    return jnp.dot(sorted_slots, integrals.T, preferred_element_type=jnp.float32)
```

```python
import functools

import jax
import jax.numpy as jnp
from jax import lax
from jax.experimental import pallas as pl
from jax.experimental.pallas import tpu as pltpu
from jax.sharding import PartitionSpec as P

VMEM_LIMIT = 48 * 1024 * 1024
NT = (((1,), (1,)), ((), ()))
SWAP = [(0, 1), (1, 0)]
NEAR = [(0, 1), (1, 0), (2, 3), (3, 2)]
MIDDLE = [(1, 2), (2, 1)]
OUTWARD = [(1, 0), (2, 3)]


def plain(amplitudes, integrals, pair_irrep, slot_irrep, owner_slot_map):
    row_count, slot_count, tile_size = amplitudes.shape
    slot_position_index = jnp.arange(slot_count, dtype=jnp.int32)
    picked = owner_slot_map[:, None] == slot_position_index[None, :]
    owner_irrep = jnp.sum(jnp.where(picked, slot_irrep[None, :], 0), axis=1)
    sorted_slots = jnp.take(amplitudes, owner_slot_map, axis=1)
    live_tiles = pair_irrep[:, None] == owner_irrep[None, :]
    sorted_slots = jnp.where(live_tiles[:, :, None], sorted_slots, jnp.zeros((), jnp.bfloat16))
    flattened = sorted_slots.reshape(row_count, slot_count * tile_size)
    columns = lax.all_to_all(flattened, "pair", split_axis=1, concat_axis=0, tiled=True)
    partial_sums = lax.dot_general(
        columns,
        lax.all_gather(integrals, "ints", axis=0, tiled=True),
        NT,
        preferred_element_type=jnp.float32,
    )
    return lax.psum_scatter(partial_sums, "pair", scatter_dimension=0, tiled=True)


def own_half_kernel(where_ref, x_ref, first_ref, second_ref):
    step = pl.program_id(0)
    per = pl.num_programs(0) // 2

    @pl.when(step < per)
    def _():
        first_ref[0] = x_ref[...]

    @pl.when(step >= per)
    def _():
        second_ref[0] = x_ref[...]


def own_half(where, integrals, tile):
    rows, columns = integrals.shape
    held, half = columns // tile, tile // 2
    per = held // 2
    chunk = jax.ShapeDtypeStruct((per, rows, half), integrals.dtype)
    return pl.pallas_call(
        own_half_kernel,
        grid_spec=pltpu.PrefetchScalarGridSpec(
            num_scalar_prefetch=1,
            grid=(held,),
            in_specs=[pl.BlockSpec((rows, half), lambda i, w: (0, 2 * i + w[1]))],
            out_specs=[
                pl.BlockSpec((1, rows, half), lambda i, w: (jnp.minimum(i, per - 1), 0, 0)),
                pl.BlockSpec((1, rows, half), lambda i, w: (jnp.maximum(i - per, 0), 0, 0)),
            ],
        ),
        out_shape=[chunk, chunk],
        cost_estimate=pl.CostEstimate(flops=0, bytes_accessed=4 * rows * columns, transcendentals=0),
        name="own_half",
    )(where, integrals)


def pack_kernel(rows, slots, where_ref, slot_irrep_ref, slot_map_ref, pair_irrep_ref, x_ref, other_ref, mine_ref, rank_ref, irrep_ref, pick_ref):
    step = pl.program_id(0)
    per = pl.num_programs(0) // 2

    @pl.when(step == 0)
    def _():
        lane = lax.broadcasted_iota(jnp.int32, (1, rows * slots), 1)
        slot_lane, row_lane = lane % slots, lane // slots
        counts = [jnp.int32(0), jnp.int32(0)]
        lane_rank = jnp.zeros_like(lane)
        lane_irrep = jnp.zeros_like(lane)
        for q in range(slots):
            slot = slot_map_ref[q]
            irrep = slot_irrep_ref[slot]
            odd = irrep == 1
            rank = jnp.where(odd, counts[1], counts[0])
            counts = [jnp.where(odd, counts[0], counts[0] + 1), jnp.where(odd, counts[1] + 1, counts[1])]
            rank_ref[q] = rank
            irrep_ref[q] = irrep
            here = slot_lane == slot
            lane_rank = jnp.where(here, rank, lane_rank)
            lane_irrep = jnp.where(here, irrep, lane_irrep)
        row_irrep = jnp.zeros_like(lane)
        for o in range(rows):
            row_irrep = jnp.where(row_lane == o, pair_irrep_ref[o], row_irrep)
        target = jnp.where(lane_irrep == row_irrep, lane_rank * rows + row_lane, -1)
        row = lax.broadcasted_iota(jnp.int32, pick_ref.shape, 0)
        pick_ref[...] = jnp.where(row == target, 1.0, 0.0).astype(pick_ref.dtype)

    packed = jnp.dot(pick_ref[...], x_ref[...], preferred_element_type=jnp.float32).astype(x_ref.dtype)

    @pl.when(step < per)
    def _():
        other_ref[...] = packed

    @pl.when(step >= per)
    def _():
        mine_ref[...] = packed


def pack(where, amplitudes, pair_irrep, slot_irrep, owner_slot_map, steps=4):
    rows, slots, tile = amplitudes.shape
    live, half, per = slots // 2, tile // 2, steps // 2
    width = tile // steps
    packed = jax.ShapeDtypeStruct((live * rows, half), amplitudes.dtype)
    tables = jax.ShapeDtypeStruct((slots,), jnp.int32)
    smem = pl.BlockSpec(memory_space=pltpu.SMEM)

    def column(i, w, *_):
        half_here = jnp.where(i < per, 1 - w[1], w[1])
        return (0, half_here * per + i % per)

    return pl.pallas_call(
        functools.partial(pack_kernel, rows, slots),
        grid_spec=pltpu.PrefetchScalarGridSpec(
            num_scalar_prefetch=4,
            grid=(steps,),
            in_specs=[pl.BlockSpec((rows * slots, width), column)],
            out_specs=[
                pl.BlockSpec((live * rows, width), lambda i, *_: (0, jnp.minimum(i, per - 1))),
                pl.BlockSpec((live * rows, width), lambda i, *_: (0, jnp.maximum(i - per, 0))),
                smem,
                smem,
            ],
            scratch_shapes=[pltpu.VMEM((live * rows, rows * slots), amplitudes.dtype)],
        ),
        out_shape=[packed, packed, tables, tables],
        compiler_params=pltpu.CompilerParams(vmem_limit_bytes=VMEM_LIMIT),
        cost_estimate=pl.CostEstimate(
            flops=2 * live * rows * rows * slots * tile, bytes_accessed=3 * rows * slots * tile, transcendentals=0
        ),
        name="pack",
    )(where, slot_irrep, owner_slot_map, pair_irrep, amplitudes.reshape(rows * slots, tile))


def sum_kernel(rows, table, counts, begun, where_ref, rank_ref, irrep_ref, *refs):
    tiles, refs = refs[:4], refs[4:]
    chunks, refs = refs[: len(counts)], refs[len(counts) :]
    if begun:
        begun_ref, out_ref, total_ref = refs
    else:
        out_ref, total_ref = refs
    total_ref[...] = jnp.zeros_like(total_ref)
    place = where_ref[0]
    entry = 0
    for chunk_ref, count in zip(chunks, counts):
        for i in range(count):
            position = jnp.int32(table[0][entry])
            for z in range(1, len(table)):
                position = jnp.where(place == z, table[z][entry], position)
            entry += 1

            @pl.when(position >= 0)
            def _():
                at = jnp.maximum(position, 0)
                start = pl.multiple_of(rank_ref[at] * rows, rows)
                here = jnp.concatenate([t[pl.ds(start, rows), :] for t in tiles], axis=0)
                term = lax.dot_general(here, chunk_ref[i], NT, preferred_element_type=jnp.float32)
                total_ref[irrep_ref[at]] += term

    out = jnp.concatenate([total_ref[0], total_ref[1]], axis=1)
    if begun:
        out = out + begun_ref[...]
    out_ref[...] = out


def add_positions(where, rank, irrep, tiles, chunks, table, begun=None, name="sum"):
    live = rank.shape[0] // 2
    rows = tiles[0].shape[0] // live
    ab = chunks[0].shape[1]
    counts = tuple(c.shape[0] for c in chunks)
    vmem = pl.BlockSpec(memory_space=pltpu.VMEM)
    smem = pl.BlockSpec(memory_space=pltpu.SMEM)
    more = [] if begun is None else [begun]
    entries = sum(counts)
    return pl.pallas_call(
        functools.partial(sum_kernel, rows, table, counts, begun is not None),
        in_specs=[smem] * 3 + [vmem] * (4 + len(chunks) + len(more)),
        out_specs=vmem,
        out_shape=jax.ShapeDtypeStruct((4 * rows, 2 * ab), jnp.float32),
        scratch_shapes=[pltpu.VMEM((2, 4 * rows, ab), jnp.float32)],
        compiler_params=pltpu.CompilerParams(vmem_limit_bytes=VMEM_LIMIT),
        cost_estimate=pl.CostEstimate(
            flops=8 * rows * ab * chunks[0].shape[2] * entries,
            bytes_accessed=2 * sum(c.size for c in chunks) + 2 * sum(t.size for t in tiles),
            transcendentals=0,
        ),
        name=name,
    )(where, rank, irrep, *tiles, *chunks, *more)


def on_line(amplitudes, integrals, pair_irrep, slot_irrep, owner_slot_map):
    rows, slots, tile = amplitudes.shape
    place, side, core = lax.axis_index("pair"), lax.axis_index("ints"), lax.axis_index("rep")
    where = jnp.stack([place, core]).astype(jnp.int32)
    across = [(i, 3 - i) for i in range(4)]
    beside = [(i, i ^ 2) for i in range(4)]

    first, second = own_half(where, integrals, tile)
    near1 = lax.ppermute(first, "pair", NEAR)
    mid1 = lax.ppermute(first, "pair", MIDDLE)
    near2 = lax.ppermute(second, "pair", NEAR)
    mid2 = lax.ppermute(second, "pair", MIDDLE)

    other, mine, rank, irrep = pack(where, amplitudes, pair_irrep, slot_irrep, owner_slot_map)
    from_core = lax.ppermute(other, "rep", SWAP)
    from_side = lax.ppermute(mine, ("ints", "rep"), beside)
    from_across = lax.ppermute(other, ("ints", "rep"), across)

    mid3 = lax.ppermute(near1, "pair", MIDDLE)
    out1 = lax.ppermute(mid1, "pair", OUTWARD)
    mid4 = lax.ppermute(near2, "pair", MIDDLE)
    out2 = lax.ppermute(mid2, "pair", OUTWARD)
    out3 = lax.ppermute(mid3, "pair", OUTWARD)
    out4 = lax.ppermute(mid4, "pair", OUTWARD)

    tiles = (mine, from_core, from_side, from_across)
    held = slots // 4
    per = held // 2

    def chunk_of(z, b):
        return list(range(z * held + b * per, z * held + b * per + per))

    none = [-1] * per
    table = []
    for z in range(4):
        near, far = z ^ 1, 3 - z
        inner = z in (1, 2)
        row = chunk_of(z, 0) + chunk_of(z, 1) + chunk_of(near, 0) + chunk_of(near, 1)
        if inner:
            row += chunk_of(far, 0) + chunk_of(far, 1) + chunk_of(far ^ 1, 0) + chunk_of(far ^ 1, 1) + none * 3
        else:
            row += none * 4 + chunk_of(far ^ 1, 0) + chunk_of(far ^ 1, 1) + chunk_of(far, 0)
        table.append(tuple(row))
    partial_sums = add_positions(
        where, rank, irrep, tiles, (first, second, near1, near2, mid1, mid2, mid3, mid4, out1, out2, out3), tuple(table), name="sum_most"
    )
    last = tuple(tuple(none if z in (1, 2) else chunk_of(3 - z, 1)) for z in range(4))
    partial_sums = add_positions(where, rank, irrep, tiles, (out4,), last, partial_sums, name="sum_last")

    blocks = [partial_sums[i * rows : (i + 1) * rows] for i in range(4)]
    own = blocks[0] + lax.ppermute(blocks[1], "rep", SWAP)
    theirs = lax.ppermute(blocks[2], ("ints", "rep"), beside) + lax.ppermute(blocks[3], ("ints", "rep"), across)
    ab = integrals.shape[0]
    odd = (pair_irrep == 1)[:, None]
    own = jnp.where(odd, own[:, ab:], own[:, :ab])
    theirs = jnp.where(odd, theirs[:, ab:], theirs[:, :ab])
    return jnp.where(side == 0, jnp.concatenate([own, theirs], axis=1), jnp.concatenate([theirs, own], axis=1))


def solution(mesh):
    placed = (
        P(("groups", "pair", "ints", "rep"), None, None),
        P(("groups", "ints"), "pair"),
        P(("groups", "pair", "ints", "rep")),
        P("groups"),
        P("groups"),
    )
    line = mesh.shape["pair"] == 4 and mesh.shape["ints"] == 2 and mesh.shape["rep"] == 2
    return jax.shard_map(
        on_line if line else plain,
        mesh=mesh,
        in_specs=placed,
        out_specs=P(("groups", "pair", "ints", "rep"), None),
        check_vma=False,
    )
```

```python
import functools

import jax
import jax.numpy as jnp
from jax import lax
from jax.experimental import pallas as pl
from jax.experimental.pallas import tpu as pltpu
from jax.sharding import PartitionSpec as P

VMEM_LIMIT = 12 * 1024 * 1024
PREPARE_VMEM = 50 * 1024 * 1024
NT = (((1,), (1,)), ((), ()))
SWAP = [(0, 1), (1, 0)]
NEAR = [(0, 1), (1, 0), (2, 3), (3, 2)]
MIDDLE = [(1, 2), (2, 1)]
OUTWARD = [(1, 0), (2, 3)]


def plain(amplitudes, integrals, pair_irrep, slot_irrep, owner_slot_map):
    row_count, slot_count, tile_size = amplitudes.shape
    slot_position_index = jnp.arange(slot_count, dtype=jnp.int32)
    picked = owner_slot_map[:, None] == slot_position_index[None, :]
    owner_irrep = jnp.sum(jnp.where(picked, slot_irrep[None, :], 0), axis=1)
    sorted_slots = jnp.take(amplitudes, owner_slot_map, axis=1)
    live_tiles = pair_irrep[:, None] == owner_irrep[None, :]
    sorted_slots = jnp.where(live_tiles[:, :, None], sorted_slots, jnp.zeros((), jnp.bfloat16))
    flattened = sorted_slots.reshape(row_count, slot_count * tile_size)
    columns = lax.all_to_all(flattened, "pair", split_axis=1, concat_axis=0, tiled=True)
    partial_sums = lax.dot_general(
        columns,
        lax.all_gather(integrals, "ints", axis=0, tiled=True),
        NT,
        preferred_element_type=jnp.float32,
    )
    return lax.psum_scatter(partial_sums, "pair", scatter_dimension=0, tiled=True)


def prepare_kernel(rows, slots, scalar_ref, x_ref, integrals_ref, other_ref, mine_ref, first_ref, second_ref, table_ref, held_ref, pick_ref, copied, loaded):
    steps, _, width = held_ref.shape
    half = first_ref.shape[2]
    core = scalar_ref[1]
    moves, loads = [], []
    for p in range(2 * first_ref.shape[0]):
        chunk_ref = first_ref if p < first_ref.shape[0] else second_ref
        start = pl.multiple_of((2 * p + core) * half, half)
        source = integrals_ref.at[:, pl.ds(start, half)]
        moves.append(pltpu.make_async_copy(source, chunk_ref.at[p % first_ref.shape[0]], copied.at[p]))
    for i in range(steps):
        half_here = core if i < steps // 2 else 1 - core
        start = pl.multiple_of(half_here * half + i % (steps // 2) * width, width)
        loads.append(pltpu.make_async_copy(x_ref.at[:, pl.ds(start, width)], held_ref.at[i], loaded.at[i]))
    for move in moves + loads:
        move.start()

    groups, picked, per_group = pick_ref.shape
    group = per_group // slots
    lane = lax.broadcasted_iota(jnp.int32, (1, per_group), 1)
    slot_lane, row_lane = lane % slots, lane // slots
    counts = [jnp.int32(0), jnp.int32(0)]
    lane_rank = jnp.zeros_like(lane)
    lane_irrep = jnp.zeros_like(lane)
    for q in range(slots):
        slot = scalar_ref[2 + slots + q]
        irrep = scalar_ref[2 + slot]
        odd = irrep == 1
        rank = jnp.where(odd, counts[1], counts[0])
        counts = [jnp.where(odd, counts[0], counts[0] + 1), jnp.where(odd, counts[1] + 1, counts[1])]
        table_ref[q] = rank
        table_ref[slots + q] = irrep
        here = slot_lane == slot
        lane_rank = jnp.where(here, rank, lane_rank)
        lane_irrep = jnp.where(here, irrep, lane_irrep)
    table_ref[2 * slots] = scalar_ref[0]
    row = lax.broadcasted_iota(jnp.int32, (picked, per_group), 0)
    for g in range(groups):
        row_irrep = jnp.zeros_like(lane)
        for o in range(group):
            row_irrep = jnp.where(row_lane == o, scalar_ref[2 + 2 * slots + g * group + o], row_irrep)
        target = jnp.where(lane_irrep == row_irrep, lane_rank * group + row_lane, -1)
        pick_ref[g] = jnp.where(row == target, 1.0, 0.0).astype(pick_ref.dtype)

    for i in range(steps):
        loads[i].wait()
        into = mine_ref if i < steps // 2 else other_ref
        at = i % (steps // 2) * width
        for g in range(groups):
            source = held_ref[i, g * per_group : (g + 1) * per_group]
            packed = jnp.dot(pick_ref[g], source, preferred_element_type=jnp.float32).astype(held_ref.dtype)
            for j in range(picked // group):
                to = j * rows + g * group
                into[to : to + group, at : at + width] = packed[j * group : (j + 1) * group]
    for move in moves:
        move.wait()


def prepare(scalars, amplitudes, integrals, steps=8):
    rows, slots, tile = amplitudes.shape
    live, half = slots // 2, tile // 2
    ab, columns = integrals.shape
    held = columns // tile
    packed = jax.ShapeDtypeStruct((live * rows, half), amplitudes.dtype)
    chunk = jax.ShapeDtypeStruct((held // 2, ab, half), integrals.dtype)
    hbm = pl.BlockSpec(memory_space=pltpu.HBM)
    vmem = pl.BlockSpec(memory_space=pltpu.VMEM)
    smem = pl.BlockSpec(memory_space=pltpu.SMEM)
    return pl.pallas_call(
        functools.partial(prepare_kernel, rows, slots),
        in_specs=[smem, hbm, hbm],
        out_specs=[vmem, vmem, vmem, vmem, smem],
        out_shape=[packed, packed, chunk, chunk, jax.ShapeDtypeStruct((2 * slots + 1,), jnp.int32)],
        scratch_shapes=[
            pltpu.VMEM((steps, rows * slots, tile // steps), amplitudes.dtype),
            pltpu.VMEM((rows // 16, live * 16, 16 * slots), amplitudes.dtype),
            pltpu.SemaphoreType.DMA((held,)),
            pltpu.SemaphoreType.DMA((steps,)),
        ],
        compiler_params=pltpu.CompilerParams(vmem_limit_bytes=PREPARE_VMEM),
        cost_estimate=pl.CostEstimate(
            flops=2 * live * rows * rows * slots * tile, bytes_accessed=3 * rows * slots * tile, transcendentals=0
        ),
        name="prepare",
    )(scalars, amplitudes.reshape(rows * slots, tile), integrals)


def sum_kernel(rows, slots, held, work, table, begun, ends, scalar_ref, *refs):
    tiles, refs = refs[:held], refs[held:]
    count = len(table)
    chunks, refs = refs[:count], refs[count:]
    total_ref = refs[-1]
    total_ref[...] = refs[0][...] if begun else jnp.zeros_like(total_ref)
    place = scalar_ref[2 * slots]
    for (low, high), used in work:
        for c in used:
            for i in range(chunks[c].shape[0]):
                position = jnp.int32(table[c][0][i])
                for z in range(1, len(table[c])):
                    position = jnp.where(place == z, table[c][z][i], position)

                @pl.when(position >= 0)
                def _():
                    at = jnp.maximum(position, 0)
                    start = pl.multiple_of(scalar_ref[at] * rows, rows)
                    here = jnp.concatenate([t[pl.ds(start, rows), :] for t in tiles[low:high]], axis=0)
                    term = lax.dot_general(here, chunks[c][i], NT, preferred_element_type=jnp.float32)
                    total_ref[scalar_ref[slots + at], low * rows : high * rows] += term

    if ends:
        for t, out_ref in enumerate(refs[-5:-1]):
            at = slice(t * rows, (t + 1) * rows)
            out_ref[...] = jnp.concatenate([total_ref[0, at], total_ref[1, at]], axis=1)


def add_positions(scalars, tiles, chunks, table, work, begun=None, ends=False, name="sum"):
    slots = scalars.shape[0] // 2
    live = slots // 2
    rows = tiles[0].shape[0] // live
    ab, half = chunks[0].shape[1:]
    vmem = pl.BlockSpec(memory_space=pltpu.VMEM)
    smem = pl.BlockSpec(memory_space=pltpu.SMEM)
    more = [] if begun is None else [begun]
    flops = sum(2 * rows * (high - low) * ab * half * chunks[c].shape[0] for (low, high), used in work for c in used)
    total = (2, 4 * rows, ab)
    return pl.pallas_call(
        functools.partial(sum_kernel, rows, slots, len(tiles), work, table, begun is not None, ends),
        in_specs=[smem] + [vmem] * (len(tiles) + len(chunks) + len(more)),
        out_specs=[vmem] * 4 if ends else vmem,
        out_shape=[jax.ShapeDtypeStruct((rows, 2 * ab), jnp.float32)] * 4 if ends else jax.ShapeDtypeStruct(total, jnp.float32),
        scratch_shapes=[pltpu.VMEM(total, jnp.float32)] if ends else [],
        compiler_params=pltpu.CompilerParams(vmem_limit_bytes=VMEM_LIMIT),
        name=name,
    )(scalars, *tiles, *chunks, *more)


def after(array, *earlier):
    return lax.optimization_barrier((array, *earlier))[0] if earlier else array


def on_line(amplitudes, integrals, pair_irrep, slot_irrep, owner_slot_map):
    rows, slots, tile = amplitudes.shape
    place, side, core = lax.axis_index("pair"), lax.axis_index("ints"), lax.axis_index("rep")
    scalars = jnp.concatenate([jnp.stack([place, core]).astype(jnp.int32), slot_irrep, owner_slot_map, pair_irrep])
    across = [(i, 3 - i) for i in range(4)]
    beside = [(i, i ^ 2) for i in range(4)]

    other, mine, first, second, scalars = prepare(scalars, amplitudes, integrals)
    held = slots // 4
    per = held // 2
    none = (-1,) * per

    def held_at(places, b):
        return tuple(none if z is None else tuple(range(z * held + b * per, z * held + b * per + per)) for z in places)

    home, near = (0, 1, 2, 3), (1, 0, 3, 2)
    middle, beyond = (None, 2, 1, None), (None, 3, 0, None)
    outer, outermost = (2, None, None, 1), (3, None, None, 0)
    chunks = {"first": (first, held_at(home, 0)), "second": (second, held_at(home, 1))}
    tiles = [mine, lax.ppermute(other, "rep", SWAP)]

    def add(name, sums, *step, ends=False):
        names = sorted({name for *_, used in step for name in used.split()})
        return add_positions(
            scalars,
            tiles[: max(high for _, high, _ in step)],
            tuple(chunks[name][0] for name in names),
            tuple(chunks[name][1] for name in names),
            tuple(((low, high), tuple(names.index(name) for name in used.split())) for low, high, used in step),
            begun=sums,
            ends=ends,
            name=name,
        )

    def send(name, source, pairs, positions, *earlier):
        chunks[name] = (lax.ppermute(after(chunks[source][0], *earlier), "pair", pairs), positions)

    send("near1", "first", NEAR, held_at(near, 0))
    send("mid1", "first", MIDDLE, held_at(middle, 0))
    tiles.append(lax.ppermute(mine, ("ints", "rep"), beside))
    send("mid2", "second", MIDDLE, held_at(middle, 1))
    sums = add("sum_0", None, (0, 2, "first second"))
    send("near2", "second", NEAR, held_at(near, 1), sums)
    send("out1", "mid1", OUTWARD, held_at(outer, 0))
    send("mid3", "near1", MIDDLE, held_at(beyond, 0))
    sums = add("sum_1", sums, (0, 2, "near1 mid1"))
    send("out2", "mid2", OUTWARD, held_at(outer, 1), sums)
    send("mid4", "near2", MIDDLE, held_at(beyond, 1), sums)
    sums = add("sum_2", sums, (0, 2, "near2 mid2"))
    sums = add("sum_3", sums, (2, 3, "first second near1 near2 mid1 mid2"))
    tiles.append(lax.ppermute(after(other, sums), ("ints", "rep"), across))
    send("out3", "mid3", OUTWARD, held_at(outermost, 0), sums)
    sums = add("sum_4", sums, (0, 3, "mid3 out1"))
    send("out4", "mid4", OUTWARD, held_at(outermost, 1), sums)
    sums = add("sum_5", sums, (0, 3, "mid4 out2"))
    sums = add("sum_6", sums, (3, 4, "first second near1 near2 mid1 mid2 mid3 mid4 out1 out2"))
    sums = add("sum_7", sums, (0, 4, "out3"))
    sums = add("sum_8", sums, (0, 4, "out4"), ends=True)

    own = sums[0] + lax.ppermute(sums[1], "rep", SWAP)
    theirs = lax.ppermute(sums[2], ("ints", "rep"), beside) + lax.ppermute(sums[3], ("ints", "rep"), across)
    ab = integrals.shape[0]
    odd = (pair_irrep == 1)[:, None]
    own = jnp.where(odd, own[:, ab:], own[:, :ab])
    theirs = jnp.where(odd, theirs[:, ab:], theirs[:, :ab])
    return jnp.where(side == 0, jnp.concatenate([own, theirs], axis=1), jnp.concatenate([theirs, own], axis=1))


def solution(mesh):
    placed = (
        P(("groups", "pair", "ints", "rep"), None, None),
        P(("groups", "ints"), "pair"),
        P(("groups", "pair", "ints", "rep")),
        P("groups"),
        P("groups"),
    )
    line = mesh.shape["pair"] == 4 and mesh.shape["ints"] == 2 and mesh.shape["rep"] == 2
    return jax.shard_map(
        on_line if line else plain,
        mesh=mesh,
        in_specs=placed,
        out_specs=P(("groups", "pair", "ints", "rep"), None),
        check_vma=False,
    )
```

```python
import functools

import jax
import jax.numpy as jnp
from jax import lax
from jax.experimental import pallas as pl
from jax.experimental.pallas import tpu as pltpu
from jax.sharding import PartitionSpec as P

VMEM_LIMIT = 12 * 1024 * 1024
PREPARE_VMEM = 50 * 1024 * 1024
NT = (((1,), (1,)), ((), ()))
SWAP = [(0, 1), (1, 0)]
NEAR = [(0, 1), (1, 0), (2, 3), (3, 2)]
MIDDLE = [(1, 2), (2, 1)]
OUTWARD = [(1, 0), (2, 3)]
INWARD = [(0, 1), (3, 2)]


def plain(amplitudes, integrals, pair_irrep, slot_irrep, owner_slot_map):
    row_count, slot_count, tile_size = amplitudes.shape
    slot_position_index = jnp.arange(slot_count, dtype=jnp.int32)
    picked = owner_slot_map[:, None] == slot_position_index[None, :]
    owner_irrep = jnp.sum(jnp.where(picked, slot_irrep[None, :], 0), axis=1)
    sorted_slots = jnp.take(amplitudes, owner_slot_map, axis=1)
    live_tiles = pair_irrep[:, None] == owner_irrep[None, :]
    sorted_slots = jnp.where(live_tiles[:, :, None], sorted_slots, jnp.zeros((), jnp.bfloat16))
    flattened = sorted_slots.reshape(row_count, slot_count * tile_size)
    columns = lax.all_to_all(flattened, "pair", split_axis=1, concat_axis=0, tiled=True)
    partial_sums = lax.dot_general(
        columns,
        lax.all_gather(integrals, "ints", axis=0, tiled=True),
        NT,
        preferred_element_type=jnp.float32,
    )
    return lax.psum_scatter(partial_sums, "pair", scatter_dimension=0, tiled=True)


def prepare_kernel(rows, slots, scalar_ref, x_ref, integrals_ref, other_ref, mine_ref, own_ref, first_ref, second_ref, table_ref, held_ref, pick_ref, copied, loaded):
    steps, _, width = held_ref.shape
    half = first_ref.shape[2]
    core = scalar_ref[1]
    moves, loads = [], []
    held = own_ref.shape[0]
    for p in range(held):
        start = pl.multiple_of((2 * p + core) * half, half)
        source = integrals_ref.at[:, pl.ds(start, half)]
        moves.append(pltpu.make_async_copy(source, own_ref.at[p], copied.at[p]))
    for i in range(steps):
        half_here = core if i < steps // 2 else 1 - core
        start = pl.multiple_of(half_here * half + i % (steps // 2) * width, width)
        loads.append(pltpu.make_async_copy(x_ref.at[:, pl.ds(start, width)], held_ref.at[i], loaded.at[i]))
    for move in moves + loads:
        move.start()

    groups, picked, per_group = pick_ref.shape
    group = per_group // slots
    lane = lax.broadcasted_iota(jnp.int32, (1, per_group), 1)
    slot_lane, row_lane = lane % slots, lane // slots
    counts = [jnp.int32(0), jnp.int32(0)]
    lane_rank = jnp.zeros_like(lane)
    lane_irrep = jnp.zeros_like(lane)
    begin = jnp.where(scalar_ref[0] < 2, slots - held, 0) + held // 2
    for q in range(slots):
        position = lax.rem(begin + q, slots)
        slot = scalar_ref[2 + slots + position]
        irrep = scalar_ref[2 + slot]
        odd = irrep == 1
        rank = jnp.where(odd, counts[1], counts[0])
        counts = [jnp.where(odd, counts[0], counts[0] + 1), jnp.where(odd, counts[1] + 1, counts[1])]
        table_ref[position] = rank
        table_ref[slots + position] = irrep
        here = slot_lane == slot
        lane_rank = jnp.where(here, rank, lane_rank)
        lane_irrep = jnp.where(here, irrep, lane_irrep)
    table_ref[2 * slots] = scalar_ref[0]
    row = lax.broadcasted_iota(jnp.int32, (picked, per_group), 0)
    for g in range(groups):
        row_irrep = jnp.zeros_like(lane)
        for o in range(group):
            row_irrep = jnp.where(row_lane == o, scalar_ref[2 + 2 * slots + g * group + o], row_irrep)
        target = jnp.where(lane_irrep == row_irrep, lane_rank * group + row_lane, -1)
        pick_ref[g] = jnp.where(row == target, 1.0, 0.0).astype(pick_ref.dtype)

    for i in range(steps):
        loads[i].wait()
        into = mine_ref if i < steps // 2 else other_ref
        at = i % (steps // 2) * width
        for g in range(groups):
            source = held_ref[i, g * per_group : (g + 1) * per_group]
            packed = jnp.dot(pick_ref[g], source, preferred_element_type=jnp.float32).astype(held_ref.dtype)
            for j in range(picked // group):
                to = j * rows + g * group
                into[to : to + group, at : at + width] = packed[j * group : (j + 1) * group]
    for p, move in enumerate(moves):
        move.wait()
        chunk_ref = first_ref if p < held // 2 else second_ref
        chunk_ref[p % (held // 2)] = own_ref[p]


def prepare(scalars, amplitudes, integrals, steps=8):
    rows, slots, tile = amplitudes.shape
    live, half = slots // 2, tile // 2
    ab, columns = integrals.shape
    held = columns // tile
    packed = jax.ShapeDtypeStruct((live * rows, half), amplitudes.dtype)
    whole = jax.ShapeDtypeStruct((held, ab, half), integrals.dtype)
    chunk = jax.ShapeDtypeStruct((held // 2, ab, half), integrals.dtype)
    hbm = pl.BlockSpec(memory_space=pltpu.HBM)
    vmem = pl.BlockSpec(memory_space=pltpu.VMEM)
    smem = pl.BlockSpec(memory_space=pltpu.SMEM)
    return pl.pallas_call(
        functools.partial(prepare_kernel, rows, slots),
        in_specs=[smem, hbm, hbm],
        out_specs=[vmem, vmem, vmem, vmem, vmem, smem],
        out_shape=[packed, packed, whole, chunk, chunk, jax.ShapeDtypeStruct((2 * slots + 1,), jnp.int32)],
        scratch_shapes=[
            pltpu.VMEM((steps, rows * slots, tile // steps), amplitudes.dtype),
            pltpu.VMEM((rows // 16, live * 16, 16 * slots), amplitudes.dtype),
            pltpu.SemaphoreType.DMA((held,)),
            pltpu.SemaphoreType.DMA((steps,)),
        ],
        compiler_params=pltpu.CompilerParams(vmem_limit_bytes=PREPARE_VMEM),
        cost_estimate=pl.CostEstimate(
            flops=2 * live * rows * rows * slots * tile, bytes_accessed=3 * rows * slots * tile, transcendentals=0
        ),
        name="prepare",
    )(scalars, amplitudes.reshape(rows * slots, tile), integrals)


def sum_kernel(rows, slots, tiles, work, table, ends, extra, scalar_ref, *refs):
    arrays, refs = refs[: tiles[-1][0] + 1], refs[tiles[-1][0] + 1 :]
    chunks, refs = refs[: len(table)], refs[len(table) :]
    total_ref = refs[-1]
    total_ref[...] = refs[0][...] if extra else jnp.zeros_like(total_ref)
    place = scalar_ref[2 * slots]
    for (low, high), used in work:
        for c in used:
            for i in range(chunks[c].shape[0]):
                position = jnp.int32(table[c][0][i])
                for z in range(1, len(table[c])):
                    position = jnp.where(place == z, table[c][z][i], position)

                @pl.when(position >= 0)
                def _():
                    at = jnp.maximum(position, 0)
                    start = scalar_ref[at] * rows
                    here = jnp.concatenate(
                        [arrays[t][pl.ds(pl.multiple_of(start + base, rows), rows), :] for t, base in tiles[low:high]], axis=0
                    )
                    term = lax.dot_general(here, chunks[c][i], NT, preferred_element_type=jnp.float32)
                    total_ref[scalar_ref[slots + at], low * rows : high * rows] += term

    if ends:
        blocks = refs[-1 - ends : -1]
        for t, out_ref in enumerate(blocks):
            size = total_ref.shape[1] // ends
            at = slice(t * size, (t + 1) * size)
            out = jnp.concatenate([total_ref[0, at], total_ref[1, at]], axis=1)
            if extra > 1 and (t + 1) * size <= refs[1].shape[0]:
                out = out + refs[1][at]
            out_ref[...] = out


def add_positions(scalars, arrays, tiles, rows, blocks, chunks, table, work, extra=(), ends=0, name="sum"):
    slots = scalars.shape[0] // 2
    ab = chunks[0].shape[1]
    vmem = pl.BlockSpec(memory_space=pltpu.VMEM)
    smem = pl.BlockSpec(memory_space=pltpu.SMEM)
    total = (2, blocks * rows, ab)
    end = jax.ShapeDtypeStruct((blocks * rows // max(ends, 1), 2 * ab), jnp.float32)
    return pl.pallas_call(
        functools.partial(sum_kernel, rows, slots, tuple(tiles), work, table, ends, len(extra)),
        in_specs=[smem] + [vmem] * (len(arrays) + len(chunks) + len(extra)),
        out_specs=[vmem] * ends if ends else vmem,
        out_shape=[end] * ends if ends else jax.ShapeDtypeStruct(total, jnp.float32),
        scratch_shapes=[pltpu.VMEM(total, jnp.float32)] if ends else [],
        compiler_params=pltpu.CompilerParams(vmem_limit_bytes=VMEM_LIMIT),
        name=name,
    )(scalars, *arrays, *chunks, *extra)


def after(array, *earlier):
    return lax.optimization_barrier((array, *earlier))[0] if earlier else array


def on_line(amplitudes, integrals, pair_irrep, slot_irrep, owner_slot_map):
    rows, slots, tile = amplitudes.shape
    place, side, core = lax.axis_index("pair"), lax.axis_index("ints"), lax.axis_index("rep")
    scalars = jnp.concatenate([jnp.stack([place, core]).astype(jnp.int32), slot_irrep, owner_slot_map, pair_irrep])
    across = [(i, 3 - i) for i in range(4)]
    beside = [(i, i ^ 2) for i in range(4)]

    other, mine, own, first, second, scalars = prepare(scalars, amplitudes, integrals)
    held = slots // 4
    per = held // 2

    def held_at(places, low=0, high=held):
        return tuple((-1,) * (high - low) if z is None else tuple(range(z * held + low, z * held + high)) for z in places)

    home, near = (0, 1, 2, 3), (1, 0, 3, 2)
    middle, beyond = (None, 2, 1, None), (None, 3, 0, None)
    outer, outermost = (2, None, None, 1), (3, None, None, 0)
    chunks = {"own": (own, held_at(home)), "own1": (first, ()), "own2": (second, ())}
    tiles = [mine, lax.ppermute(other, "rep", SWAP)]

    def add(name, *step, arrays=None, at=None, blocks=4, extra=(), ends=0):
        names = []
        for *_, used in step:
            names += [n for n in used if n not in names]
        if arrays is None:
            arrays = tiles[: max(high for _, high, _ in step)]
            at = [(t, 0) for t in range(len(arrays))]
        return add_positions(
            scalars,
            arrays,
            at,
            rows,
            blocks,
            tuple(chunks[n][0] for n in names),
            tuple(chunks[n][1] for n in names),
            tuple(((low, high), tuple(names.index(n) for n in used)) for low, high, used in step),
            extra=extra,
            ends=ends,
            name=name,
        )

    def send(name, source, pairs, positions, *earlier):
        chunks[name] = (lax.ppermute(after(chunks[source][0], *earlier), "pair", pairs), positions)

    send("near1", "own1", NEAR, held_at(near, 0, per))
    send("mid", "own", MIDDLE, held_at(middle))
    send("near2", "own2", NEAR, held_at(near, per))
    tiles.append(lax.ppermute(mine, ("ints", "rep"), beside))
    sums = add("sum_home", (0, 2, ("own",)))
    tiles.append(lax.ppermute(after(other, sums), ("ints", "rep"), across))
    send("mid3", "near1", MIDDLE, held_at(beyond, 0, per))
    send("out", "mid", OUTWARD, held_at(outer))
    send("mid4", "near2", MIDDLE, held_at(beyond, per))
    sums = add("sum_near", (0, 2, ("near1", "near2", "mid")), extra=(sums,))
    sums = add("sum_side", (2, 3, ("own", "near1", "near2", "mid")), extra=(sums,))
    heads = lax.ppermute(after(jnp.concatenate([t[: per * rows] for t in tiles[:3]]), sums), "pair", INWARD)
    send("out3", "mid3", OUTWARD, held_at(outermost, 0, per))
    sums = add("sum_beyond", (0, 3, ("mid3", "mid4")), extra=(sums,))
    away = add("sum_away", (0, 3, ("mid4",)), arrays=[after(heads, sums)], at=[(0, t * per * rows) for t in range(3)], blocks=3, ends=1)
    back = lax.ppermute(away[0], "pair", OUTWARD)
    last_heads = lax.ppermute(tiles[3][: per * rows], "pair", INWARD)
    sums = add("sum_outer", (0, 3, ("out",)), extra=(sums,))
    everything = ("own", "near1", "near2", "mid", "mid3", "mid4", "out")
    sums = add("sum_across", (3, 4, everything), extra=(sums,))
    away = add("sum_away_across", (0, 1, ("mid4",)), arrays=[last_heads], at=[(0, 0)], blocks=1, ends=1)
    home_pairs = [(4 * a + i, 4 * b + 3 - i) for a, b in OUTWARD for i in range(4)]
    back_across = lax.ppermute(away[0], ("pair", "ints", "rep"), home_pairs)
    sums = add("sum_last", (0, 4, ("out3",)), extra=(after(sums, away[0]), back), ends=4)

    own = sums[0] + lax.ppermute(sums[1], "rep", SWAP)
    theirs = lax.ppermute(sums[2], ("ints", "rep"), beside) + lax.ppermute(sums[3], ("ints", "rep"), across)
    theirs = theirs + back_across
    ab = integrals.shape[0]
    odd = (pair_irrep == 1)[:, None]
    own = jnp.where(odd, own[:, ab:], own[:, :ab])
    theirs = jnp.where(odd, theirs[:, ab:], theirs[:, :ab])
    return jnp.where(side == 0, jnp.concatenate([own, theirs], axis=1), jnp.concatenate([theirs, own], axis=1))


def solution(mesh):
    placed = (
        P(("groups", "pair", "ints", "rep"), None, None),
        P(("groups", "ints"), "pair"),
        P(("groups", "pair", "ints", "rep")),
        P("groups"),
        P("groups"),
    )
    line = mesh.shape["pair"] == 4 and mesh.shape["ints"] == 2 and mesh.shape["rep"] == 2
    return jax.shard_map(
        on_line if line else plain,
        mesh=mesh,
        in_specs=placed,
        out_specs=P(("groups", "pair", "ints", "rep"), None),
        check_vma=False,
    )
```

```python
import functools

import jax
import jax.numpy as jnp
from jax import lax
from jax.experimental import pallas as pl
from jax.experimental.pallas import tpu as pltpu
from jax.sharding import PartitionSpec as P

VMEM_LIMIT = 12 * 1024 * 1024
OWN_VMEM = 52 * 1024 * 1024
NT = (((1,), (1,)), ((), ()))
SWAP = [(0, 1), (1, 0)]
NEAR = [(0, 1), (1, 0), (2, 3), (3, 2)]
MIDDLE = [(1, 2), (2, 1)]
OUTWARD = [(1, 0), (2, 3)]
INWARD = [(0, 1), (3, 2)]


def plain(amplitudes, integrals, pair_irrep, slot_irrep, owner_slot_map):
    row_count, slot_count, tile_size = amplitudes.shape
    slot_position_index = jnp.arange(slot_count, dtype=jnp.int32)
    picked = owner_slot_map[:, None] == slot_position_index[None, :]
    owner_irrep = jnp.sum(jnp.where(picked, slot_irrep[None, :], 0), axis=1)
    sorted_slots = jnp.take(amplitudes, owner_slot_map, axis=1)
    live_tiles = pair_irrep[:, None] == owner_irrep[None, :]
    sorted_slots = jnp.where(live_tiles[:, :, None], sorted_slots, jnp.zeros((), jnp.bfloat16))
    flattened = sorted_slots.reshape(row_count, slot_count * tile_size)
    columns = lax.all_to_all(flattened, "pair", split_axis=1, concat_axis=0, tiled=True)
    partial_sums = lax.dot_general(
        columns,
        lax.all_gather(integrals, "ints", axis=0, tiled=True),
        NT,
        preferred_element_type=jnp.float32,
    )
    return lax.psum_scatter(partial_sums, "pair", scatter_dimension=0, tiled=True)


def own_half_kernel(integrals_ref, own_ref, copied):
    held, _, half = own_ref.shape
    core = lax.axis_index("rep")
    moves = []
    for p in range(held):
        start = pl.multiple_of((2 * p + core) * half, half)
        moves.append(pltpu.make_async_copy(integrals_ref.at[:, pl.ds(start, half)], own_ref.at[p], copied.at[p]))
    for move in moves:
        move.start()
    for move in moves:
        move.wait()


def own_half(integrals, tile):
    ab, columns = integrals.shape
    held, half = columns // tile, tile // 2
    return pl.pallas_call(
        own_half_kernel,
        in_specs=[pl.BlockSpec(memory_space=pltpu.HBM)],
        out_specs=pl.BlockSpec(memory_space=pltpu.VMEM),
        out_shape=jax.ShapeDtypeStruct((held, ab, half), integrals.dtype),
        scratch_shapes=[pltpu.SemaphoreType.DMA((held,))],
        compiler_params=pltpu.CompilerParams(vmem_limit_bytes=OWN_VMEM),
        name="own_half",
    )(integrals)


def pack_kernel(rows, slots, held, width, scalar_ref, x_ref, other_ref, mine_ref, table_ref, pick_ref):
    half = mine_ref.shape[1]
    core = scalar_ref[1]
    groups, picked, per_group = pick_ref.shape
    group = per_group // slots
    lane = lax.broadcasted_iota(jnp.int32, (1, per_group), 1)
    slot_lane, row_lane = lane % slots, lane // slots
    counts = [jnp.int32(0), jnp.int32(0)]
    lane_rank = jnp.zeros_like(lane)
    lane_irrep = jnp.zeros_like(lane)
    begin = jnp.where(scalar_ref[0] < 2, slots - held, 0) + held // 2
    for q in range(slots):
        position = lax.rem(begin + q, slots)
        slot = scalar_ref[2 + slots + position]
        irrep = scalar_ref[2 + slot]
        odd = irrep == 1
        rank = jnp.where(odd, counts[1], counts[0])
        counts = [jnp.where(odd, counts[0], counts[0] + 1), jnp.where(odd, counts[1] + 1, counts[1])]
        table_ref[position] = rank
        table_ref[slots + position] = irrep
        here = slot_lane == slot
        lane_rank = jnp.where(here, rank, lane_rank)
        lane_irrep = jnp.where(here, irrep, lane_irrep)
    table_ref[2 * slots] = scalar_ref[0]
    row = lax.broadcasted_iota(jnp.int32, (picked, per_group), 0)
    for g in range(groups):
        row_irrep = jnp.zeros_like(lane)
        for o in range(group):
            row_irrep = jnp.where(row_lane == o, scalar_ref[2 + 2 * slots + g * group + o], row_irrep)
        target = jnp.where(lane_irrep == row_irrep, lane_rank * group + row_lane, -1)
        pick_ref[g] = jnp.where(row == target, 1.0, 0.0).astype(pick_ref.dtype)

    for i in range(2 * half // width):
        into = mine_ref if i < half // width else other_ref
        at = i % (half // width) * width
        start = pl.multiple_of((core if i < half // width else 1 - core) * half + at, width)
        for g in range(groups):
            source = x_ref[g * per_group : (g + 1) * per_group, pl.ds(start, width)]
            packed = jnp.dot(pick_ref[g], source, preferred_element_type=jnp.float32).astype(x_ref.dtype)
            for j in range(picked // group):
                to = j * rows + g * group
                into[to : to + group, at : at + width] = packed[j * group : (j + 1) * group]


def pack(scalars, amplitudes, held):
    rows, slots, tile = amplitudes.shape
    live, half = slots // 2, tile // 2
    packed = jax.ShapeDtypeStruct((live * rows, half), amplitudes.dtype)
    vmem = pl.BlockSpec(memory_space=pltpu.VMEM)
    smem = pl.BlockSpec(memory_space=pltpu.SMEM)
    return pl.pallas_call(
        functools.partial(pack_kernel, rows, slots, held, half // 4),
        in_specs=[smem, vmem],
        out_specs=[vmem, vmem, smem],
        out_shape=[packed, packed, jax.ShapeDtypeStruct((2 * slots + 1,), jnp.int32)],
        scratch_shapes=[pltpu.VMEM((rows // 16, live * 16, 16 * slots), amplitudes.dtype)],
        compiler_params=pltpu.CompilerParams(vmem_limit_bytes=VMEM_LIMIT),
        name="pack",
    )(scalars, amplitudes.reshape(rows * slots, tile))


def sum_kernel(rows, slots, tiles, work, table, ends, extra, scalar_ref, *refs):
    arrays, refs = refs[: tiles[-1][0] + 1], refs[tiles[-1][0] + 1 :]
    chunks, refs = refs[: len(table)], refs[len(table) :]
    total_ref = refs[-1]
    total_ref[...] = refs[0][...] if extra else jnp.zeros_like(total_ref)
    place = scalar_ref[2 * slots]
    for (low, high), used in work:
        for c in used:
            for i in range(chunks[c].shape[0]):
                position = jnp.int32(table[c][0][i])
                for z in range(1, len(table[c])):
                    position = jnp.where(place == z, table[c][z][i], position)

                @pl.when(position >= 0)
                def _():
                    at = jnp.maximum(position, 0)
                    start = scalar_ref[at] * rows
                    here = jnp.concatenate(
                        [arrays[t][pl.ds(pl.multiple_of(start + base, rows), rows), :] for t, base in tiles[low:high]], axis=0
                    )
                    term = lax.dot_general(here, chunks[c][i], NT, preferred_element_type=jnp.float32)
                    total_ref[scalar_ref[slots + at], low * rows : high * rows] += term

    if ends:
        blocks = refs[-1 - ends : -1]
        for t, out_ref in enumerate(blocks):
            size = total_ref.shape[1] // ends
            at = slice(t * size, (t + 1) * size)
            out = jnp.concatenate([total_ref[0, at], total_ref[1, at]], axis=1)
            if extra > 1 and (t + 1) * size <= refs[1].shape[0]:
                out = out + refs[1][at]
            out_ref[...] = out


def add_positions(scalars, arrays, tiles, rows, blocks, chunks, table, work, extra=(), ends=0, name="sum"):
    slots = scalars.shape[0] // 2
    ab = chunks[0].shape[1]
    vmem = pl.BlockSpec(memory_space=pltpu.VMEM)
    smem = pl.BlockSpec(memory_space=pltpu.SMEM)
    total = (2, blocks * rows, ab)
    end = jax.ShapeDtypeStruct((blocks * rows // max(ends, 1), 2 * ab), jnp.float32)
    return pl.pallas_call(
        functools.partial(sum_kernel, rows, slots, tuple(tiles), work, table, ends, len(extra)),
        in_specs=[smem] + [vmem] * (len(arrays) + len(chunks) + len(extra)),
        out_specs=[vmem] * ends if ends else vmem,
        out_shape=[end] * ends if ends else jax.ShapeDtypeStruct(total, jnp.float32),
        scratch_shapes=[pltpu.VMEM(total, jnp.float32)] if ends else [],
        compiler_params=pltpu.CompilerParams(vmem_limit_bytes=VMEM_LIMIT),
        name=name,
    )(scalars, *arrays, *chunks, *extra)


def after(array, *earlier):
    return lax.optimization_barrier((array, *earlier))[0] if earlier else array


def on_line(amplitudes, integrals, pair_irrep, slot_irrep, owner_slot_map):
    rows, slots, tile = amplitudes.shape
    place, side, core = lax.axis_index("pair"), lax.axis_index("ints"), lax.axis_index("rep")
    scalars = jnp.concatenate([jnp.stack([place, core]).astype(jnp.int32), slot_irrep, owner_slot_map, pair_irrep])
    across = [(i, 3 - i) for i in range(4)]
    beside = [(i, i ^ 2) for i in range(4)]

    own = own_half(integrals, tile)
    other, mine, scalars = pack(after(scalars, own), amplitudes, integrals.shape[1] // tile)
    held = slots // 4
    per = held // 2

    def held_at(places, low=0, high=held):
        return tuple((-1,) * (high - low) if z is None else tuple(range(z * held + low, z * held + high)) for z in places)

    home, near = (0, 1, 2, 3), (1, 0, 3, 2)
    middle, beyond = (None, 2, 1, None), (None, 3, 0, None)
    outer, outermost = (2, None, None, 1), (3, None, None, 0)
    chunks = {"own": (own, held_at(home))}
    tiles = [mine, lax.ppermute(other, "rep", SWAP)]

    def add(name, *step, arrays=None, at=None, blocks=4, extra=(), ends=0):
        names = []
        for *_, used in step:
            names += [n for n in used if n not in names]
        if arrays is None:
            arrays = tiles[: max(high for _, high, _ in step)]
            at = [(t, 0) for t in range(len(arrays))]
        return add_positions(
            scalars,
            arrays,
            at,
            rows,
            blocks,
            tuple(chunks[n][0] for n in names),
            tuple(chunks[n][1] for n in names),
            tuple(((low, high), tuple(names.index(n) for n in used)) for low, high, used in step),
            extra=extra,
            ends=ends,
            name=name,
        )

    def send(name, array, pairs, positions, *earlier):
        chunks[name] = (lax.ppermute(after(array, *earlier), "pair", pairs), positions)
        return chunks[name][0]

    low = per * rows
    near_chunk = send("near", own, NEAR, held_at(near))
    mid_chunk = send("mid", own, MIDDLE, held_at(middle))
    tiles.append(lax.ppermute(mine, ("ints", "rep"), beside))
    tiles.append(lax.ppermute(other, ("ints", "rep"), across))
    mid3_chunk = send("mid3", near_chunk[:per], MIDDLE, held_at(beyond, 0, per))
    send("out", mid_chunk, OUTWARD, held_at(outer))
    send("mid4", near_chunk[per:], MIDDLE, held_at(beyond, per))
    first = ("own", "mid", "near")
    sums = add("sum_near", (0, 1, first))
    sums = add("sum_side", (1, 3, first), extra=(sums,))
    heads = jnp.concatenate([t[:low] for t in tiles[:3]])
    heads = lax.ppermute(after(heads, sums), "pair", INWARD)
    send("out3", mid3_chunk, OUTWARD, held_at(outermost, 0, per), sums)
    last_heads = lax.ppermute(tiles[3][:low], "pair", INWARD)
    sums = add("sum_across", (3, 4, first), extra=(sums,))
    rows_at = [(0, t * low) for t in range(3)]
    away = add("sum_away", (0, 3, ("mid4",)), arrays=[after(heads, sums)], at=rows_at, blocks=3, ends=1)
    back = lax.ppermute(away[0], "pair", OUTWARD)
    sums = add("sum_beyond", (0, 4, ("mid3", "mid4", "out")), extra=(sums,))
    away = add("sum_last_away", (0, 1, ("mid4",)), arrays=[after(last_heads, sums)], at=[(0, 0)], blocks=1, ends=1)
    home_pairs = [(4 * a + i, 4 * b + 3 - i) for a, b in OUTWARD for i in range(4)]
    back_across = lax.ppermute(away[0], ("pair", "ints", "rep"), home_pairs)
    sums = add("sum_last", (0, 4, ("out3",)), extra=(after(sums, away[0]), back), ends=4)

    own = sums[0] + lax.ppermute(sums[1], "rep", SWAP)
    theirs = lax.ppermute(sums[2], ("ints", "rep"), beside) + lax.ppermute(sums[3], ("ints", "rep"), across)
    theirs = theirs + back_across
    ab = integrals.shape[0]
    odd = (pair_irrep == 1)[:, None]
    own = jnp.where(odd, own[:, ab:], own[:, :ab])
    theirs = jnp.where(odd, theirs[:, ab:], theirs[:, :ab])
    return jnp.where(side == 0, jnp.concatenate([own, theirs], axis=1), jnp.concatenate([theirs, own], axis=1))


def solution(mesh):
    placed = (
        P(("groups", "pair", "ints", "rep"), None, None),
        P(("groups", "ints"), "pair"),
        P(("groups", "pair", "ints", "rep")),
        P("groups"),
        P("groups"),
    )
    line = mesh.shape["pair"] == 4 and mesh.shape["ints"] == 2 and mesh.shape["rep"] == 2
    return jax.shard_map(
        on_line if line else plain,
        mesh=mesh,
        in_specs=placed,
        out_specs=P(("groups", "pair", "ints", "rep"), None),
        check_vma=False,
    )
```

```python
import functools

import jax
import jax.numpy as jnp
from jax import lax
from jax.experimental import pallas as pl
from jax.experimental.pallas import tpu as pltpu
from jax.sharding import PartitionSpec as P

VMEM_LIMIT = 12 * 1024 * 1024
OWN_VMEM = 52 * 1024 * 1024
NT = (((1,), (1,)), ((), ()))
SWAP = [(0, 1), (1, 0)]
NEAR = [(0, 1), (1, 0), (2, 3), (3, 2)]
MIDDLE = [(1, 2), (2, 1)]
OUTWARD = [(1, 0), (2, 3)]
INWARD = [(0, 1), (3, 2)]


def plain(amplitudes, integrals, pair_irrep, slot_irrep, owner_slot_map):
    row_count, slot_count, tile_size = amplitudes.shape
    slot_position_index = jnp.arange(slot_count, dtype=jnp.int32)
    picked = owner_slot_map[:, None] == slot_position_index[None, :]
    owner_irrep = jnp.sum(jnp.where(picked, slot_irrep[None, :], 0), axis=1)
    sorted_slots = jnp.take(amplitudes, owner_slot_map, axis=1)
    live_tiles = pair_irrep[:, None] == owner_irrep[None, :]
    sorted_slots = jnp.where(live_tiles[:, :, None], sorted_slots, jnp.zeros((), jnp.bfloat16))
    flattened = sorted_slots.reshape(row_count, slot_count * tile_size)
    columns = lax.all_to_all(flattened, "pair", split_axis=1, concat_axis=0, tiled=True)
    partial_sums = lax.dot_general(
        columns,
        lax.all_gather(integrals, "ints", axis=0, tiled=True),
        NT,
        preferred_element_type=jnp.float32,
    )
    return lax.psum_scatter(partial_sums, "pair", scatter_dimension=0, tiled=True)


def own_half_kernel(integrals_ref, own_ref, copied):
    held, _, half = own_ref.shape
    core = lax.axis_index("rep")
    moves = []
    for p in range(held):
        start = pl.multiple_of((2 * p + core) * half, half)
        moves.append(pltpu.make_async_copy(integrals_ref.at[:, pl.ds(start, half)], own_ref.at[p], copied.at[p]))
    for move in moves:
        move.start()
    for move in moves:
        move.wait()


def own_half(integrals, tile):
    ab, columns = integrals.shape
    held, half = columns // tile, tile // 2
    return pl.pallas_call(
        own_half_kernel,
        in_specs=[pl.BlockSpec(memory_space=pltpu.HBM)],
        out_specs=pl.BlockSpec(memory_space=pltpu.VMEM),
        out_shape=jax.ShapeDtypeStruct((held, ab, half), integrals.dtype),
        scratch_shapes=[pltpu.SemaphoreType.DMA((held,))],
        compiler_params=pltpu.CompilerParams(vmem_limit_bytes=OWN_VMEM),
        name="own_half",
    )(integrals)


def pack_kernel(rows, slots, held, width, scalar_ref, x_ref, other_ref, mine_ref, table_ref, pick_ref):
    half = mine_ref.shape[1]
    core = scalar_ref[1]
    groups, picked, per_group = pick_ref.shape
    group = per_group // slots
    lane = lax.broadcasted_iota(jnp.int32, (1, per_group), 1)
    slot_lane, row_lane = lane % slots, lane // slots
    counts = [jnp.int32(0), jnp.int32(0)]
    lane_rank = jnp.zeros_like(lane)
    lane_irrep = jnp.zeros_like(lane)
    begin = jnp.where(scalar_ref[0] < 2, slots - held, 0) + held // 2
    for q in range(slots):
        position = lax.rem(begin + q, slots)
        slot = scalar_ref[2 + slots + position]
        irrep = scalar_ref[2 + slot]
        odd = irrep == 1
        rank = jnp.where(odd, counts[1], counts[0])
        counts = [jnp.where(odd, counts[0], counts[0] + 1), jnp.where(odd, counts[1] + 1, counts[1])]
        table_ref[position] = rank
        table_ref[slots + position] = irrep
        here = slot_lane == slot
        lane_rank = jnp.where(here, rank, lane_rank)
        lane_irrep = jnp.where(here, irrep, lane_irrep)
    table_ref[2 * slots] = scalar_ref[0]
    row = lax.broadcasted_iota(jnp.int32, (picked, per_group), 0)
    for g in range(groups):
        row_irrep = jnp.zeros_like(lane)
        for o in range(group):
            row_irrep = jnp.where(row_lane == o, scalar_ref[2 + 2 * slots + g * group + o], row_irrep)
        target = jnp.where(lane_irrep == row_irrep, lane_rank * group + row_lane, -1)
        pick_ref[g] = jnp.where(row == target, 1.0, 0.0).astype(pick_ref.dtype)

    for i in range(2 * half // width):
        into = mine_ref if i < half // width else other_ref
        at = i % (half // width) * width
        start = pl.multiple_of((core if i < half // width else 1 - core) * half + at, width)
        for g in range(groups):
            source = x_ref[g * per_group : (g + 1) * per_group, pl.ds(start, width)]
            packed = jnp.dot(pick_ref[g], source, preferred_element_type=jnp.float32).astype(x_ref.dtype)
            for j in range(picked // group):
                to = j * rows + g * group
                into[to : to + group, at : at + width] = packed[j * group : (j + 1) * group]


def pack(scalars, amplitudes, held):
    rows, slots, tile = amplitudes.shape
    live, half = slots // 2, tile // 2
    packed = jax.ShapeDtypeStruct((live * rows, half), amplitudes.dtype)
    vmem = pl.BlockSpec(memory_space=pltpu.VMEM)
    smem = pl.BlockSpec(memory_space=pltpu.SMEM)
    return pl.pallas_call(
        functools.partial(pack_kernel, rows, slots, held, half // 4),
        in_specs=[smem, vmem],
        out_specs=[vmem, vmem, smem],
        out_shape=[packed, packed, jax.ShapeDtypeStruct((2 * slots + 1,), jnp.int32)],
        scratch_shapes=[pltpu.VMEM((rows // 16, live * 16, 16 * slots), amplitudes.dtype)],
        compiler_params=pltpu.CompilerParams(vmem_limit_bytes=VMEM_LIMIT),
        name="pack",
    )(scalars, amplitudes.reshape(rows * slots, tile))


def sum_kernel(rows, slots, tiles, work, table, ends, extra, scalar_ref, *refs):
    arrays, refs = refs[: tiles[-1][0] + 1], refs[tiles[-1][0] + 1 :]
    chunks, refs = refs[: len(table)], refs[len(table) :]
    total_ref = refs[-1]
    total_ref[...] = refs[0][...] if extra else jnp.zeros_like(total_ref)
    place = scalar_ref[2 * slots]
    for (low, high), used in work:
        for c in used:
            for i in range(chunks[c].shape[0]):
                position = jnp.int32(table[c][0][i])
                for z in range(1, len(table[c])):
                    position = jnp.where(place == z, table[c][z][i], position)

                @pl.when(position >= 0)
                def _():
                    at = jnp.maximum(position, 0)
                    start = scalar_ref[at] * rows
                    here = jnp.concatenate(
                        [arrays[t][pl.ds(pl.multiple_of(start + base, rows), rows), :] for t, base in tiles[low:high]], axis=0
                    )
                    term = lax.dot_general(here, chunks[c][i], NT, preferred_element_type=jnp.float32)
                    total_ref[scalar_ref[slots + at], low * rows : high * rows] += term

    if ends:
        blocks = refs[-1 - ends : -1]
        for t, out_ref in enumerate(blocks):
            size = total_ref.shape[1] // ends
            at = slice(t * size, (t + 1) * size)
            out = jnp.concatenate([total_ref[0, at], total_ref[1, at]], axis=1)
            if extra > 1 and (t + 1) * size <= refs[1].shape[0]:
                out = out + refs[1][at]
            out_ref[...] = out


def add_positions(scalars, arrays, tiles, rows, blocks, chunks, table, work, extra=(), ends=0, name="sum"):
    slots = scalars.shape[0] // 2
    ab = chunks[0].shape[1]
    vmem = pl.BlockSpec(memory_space=pltpu.VMEM)
    smem = pl.BlockSpec(memory_space=pltpu.SMEM)
    total = (2, blocks * rows, ab)
    end = jax.ShapeDtypeStruct((blocks * rows // max(ends, 1), 2 * ab), jnp.float32)
    return pl.pallas_call(
        functools.partial(sum_kernel, rows, slots, tuple(tiles), work, table, ends, len(extra)),
        in_specs=[smem] + [vmem] * (len(arrays) + len(chunks) + len(extra)),
        out_specs=[vmem] * ends if ends else vmem,
        out_shape=[end] * ends if ends else jax.ShapeDtypeStruct(total, jnp.float32),
        scratch_shapes=[pltpu.VMEM(total, jnp.float32)] if ends else [],
        compiler_params=pltpu.CompilerParams(vmem_limit_bytes=VMEM_LIMIT),
        cost_estimate=pl.CostEstimate(flops=0, bytes_accessed=1 << 22, transcendentals=0),
        name=name,
    )(scalars, *arrays, *chunks, *extra)


def after(array, *earlier):
    return lax.optimization_barrier((array, *earlier))[0] if earlier else array


def on_line(amplitudes, integrals, pair_irrep, slot_irrep, owner_slot_map):
    rows, slots, tile = amplitudes.shape
    place, side, core = lax.axis_index("pair"), lax.axis_index("ints"), lax.axis_index("rep")
    scalars = jnp.concatenate([jnp.stack([place, core]).astype(jnp.int32), slot_irrep, owner_slot_map, pair_irrep])
    across = [(i, 3 - i) for i in range(4)]
    beside = [(i, i ^ 2) for i in range(4)]

    own = own_half(integrals, tile)
    other, mine, scalars = pack(after(scalars, own), amplitudes, integrals.shape[1] // tile)
    held = slots // 4
    per = held // 2

    def held_at(places, low=0, high=held):
        return tuple((-1,) * (high - low) if z is None else tuple(range(z * held + low, z * held + high)) for z in places)

    home, near = (0, 1, 2, 3), (1, 0, 3, 2)
    middle, beyond = (None, 2, 1, None), (None, 3, 0, None)
    outer, outermost = (2, None, None, 1), (3, None, None, 0)
    chunks = {"own": (own, held_at(home))}
    tiles = [mine, lax.ppermute(other, "rep", SWAP)]

    def add(name, *step, arrays=None, at=None, blocks=4, extra=(), ends=0):
        names = []
        for *_, used in step:
            names += [n for n in used if n not in names]
        if arrays is None:
            arrays = tiles[: max(high for _, high, _ in step)]
            at = [(t, 0) for t in range(len(arrays))]
        return add_positions(
            scalars,
            arrays,
            at,
            rows,
            blocks,
            tuple(chunks[n][0] for n in names),
            tuple(chunks[n][1] for n in names),
            tuple(((low, high), tuple(names.index(n) for n in used)) for low, high, used in step),
            extra=extra,
            ends=ends,
            name=name,
        )

    def send(name, array, pairs, positions, *earlier):
        chunks[name] = (lax.ppermute(after(array, *earlier), "pair", pairs), positions)
        return chunks[name][0]

    low = per * rows
    near_chunk = send("near", own, NEAR, held_at(near))
    mid_chunk = send("mid", own, MIDDLE, held_at(middle))
    tiles.append(lax.ppermute(mine, ("ints", "rep"), beside))
    tiles.append(lax.ppermute(other, ("ints", "rep"), across))
    mid3_chunk = send("mid3", near_chunk[:per], MIDDLE, held_at(beyond, 0, per))
    send("out", mid_chunk, OUTWARD, held_at(outer))
    send("mid4", near_chunk[per:], MIDDLE, held_at(beyond, per))
    first = ("own", "mid", "near")
    sums = add("sum_near", (0, 1, first))
    sums = add("sum_side", (1, 3, first), extra=(sums,))
    heads = jnp.concatenate([t[:low] for t in tiles[:3]])
    heads = lax.ppermute(after(heads, sums), "pair", INWARD)
    send("out3", mid3_chunk, OUTWARD, held_at(outermost, 0, per), sums)
    last_heads = lax.ppermute(tiles[3][:low], "pair", INWARD)
    rows_at = [(0, t * low) for t in range(3)]
    away = add("sum_away", (0, 3, ("mid4",)), arrays=[after(heads, sums)], at=rows_at, blocks=3, ends=1)
    back = lax.ppermute(away[0], "pair", OUTWARD)
    sums = add("sum_most", (3, 4, first), (0, 4, ("mid3", "mid4", "out")), extra=(after(sums, away[0]),))
    away = add("sum_last_away", (0, 1, ("mid4",)), arrays=[after(last_heads, sums)], at=[(0, 0)], blocks=1, ends=1)
    home_pairs = [(4 * a + i, 4 * b + 3 - i) for a, b in OUTWARD for i in range(4)]
    back_across = lax.ppermute(away[0], ("pair", "ints", "rep"), home_pairs)
    sums = add("sum_last", (0, 4, ("out3",)), extra=(after(sums, away[0]), back), ends=4)

    own = sums[0] + lax.ppermute(sums[1], "rep", SWAP)
    theirs = lax.ppermute(sums[2], ("ints", "rep"), beside) + lax.ppermute(sums[3], ("ints", "rep"), across)
    theirs = theirs + back_across
    ab = integrals.shape[0]
    odd = (pair_irrep == 1)[:, None]
    own = jnp.where(odd, own[:, ab:], own[:, :ab])
    theirs = jnp.where(odd, theirs[:, ab:], theirs[:, :ab])
    return jnp.where(side == 0, jnp.concatenate([own, theirs], axis=1), jnp.concatenate([theirs, own], axis=1))


def solution(mesh):
    placed = (
        P(("groups", "pair", "ints", "rep"), None, None),
        P(("groups", "ints"), "pair"),
        P(("groups", "pair", "ints", "rep")),
        P("groups"),
        P("groups"),
    )
    line = mesh.shape["pair"] == 4 and mesh.shape["ints"] == 2 and mesh.shape["rep"] == 2
    return jax.shard_map(
        on_line if line else plain,
        mesh=mesh,
        in_specs=placed,
        out_specs=P(("groups", "pair", "ints", "rep"), None),
        check_vma=False,
    )
```

```python
import functools

import jax
import jax.numpy as jnp
from jax import lax
from jax.experimental import pallas as pl
from jax.experimental.pallas import tpu as pltpu
from jax.sharding import PartitionSpec as P

VMEM_LIMIT = 12 * 1024 * 1024
OWN_VMEM = 52 * 1024 * 1024
NT = (((1,), (1,)), ((), ()))
SWAP = [(0, 1), (1, 0)]
NEAR = [(0, 1), (1, 0), (2, 3), (3, 2)]
MIDDLE = [(1, 2), (2, 1)]
OUTWARD = [(1, 0), (2, 3)]
INWARD = [(0, 1), (3, 2)]


def plain(amplitudes, integrals, pair_irrep, slot_irrep, owner_slot_map):
    row_count, slot_count, tile_size = amplitudes.shape
    slot_position_index = jnp.arange(slot_count, dtype=jnp.int32)
    picked = owner_slot_map[:, None] == slot_position_index[None, :]
    owner_irrep = jnp.sum(jnp.where(picked, slot_irrep[None, :], 0), axis=1)
    sorted_slots = jnp.take(amplitudes, owner_slot_map, axis=1)
    live_tiles = pair_irrep[:, None] == owner_irrep[None, :]
    sorted_slots = jnp.where(live_tiles[:, :, None], sorted_slots, jnp.zeros((), jnp.bfloat16))
    flattened = sorted_slots.reshape(row_count, slot_count * tile_size)
    columns = lax.all_to_all(flattened, "pair", split_axis=1, concat_axis=0, tiled=True)
    partial_sums = lax.dot_general(
        columns,
        lax.all_gather(integrals, "ints", axis=0, tiled=True),
        NT,
        preferred_element_type=jnp.float32,
    )
    return lax.psum_scatter(partial_sums, "pair", scatter_dimension=0, tiled=True)


def own_half_kernel(integrals_ref, own_ref, copied):
    held, _, half = own_ref.shape
    core = lax.axis_index("rep")
    moves = []
    for p in range(held):
        start = pl.multiple_of((2 * p + core) * half, half)
        moves.append(pltpu.make_async_copy(integrals_ref.at[:, pl.ds(start, half)], own_ref.at[p], copied.at[p]))
    for move in moves:
        move.start()
    for move in moves:
        move.wait()


def own_half(integrals, tile):
    ab, columns = integrals.shape
    held, half = columns // tile, tile // 2
    return pl.pallas_call(
        own_half_kernel,
        in_specs=[pl.BlockSpec(memory_space=pltpu.HBM)],
        out_specs=pl.BlockSpec(memory_space=pltpu.VMEM),
        out_shape=jax.ShapeDtypeStruct((held, ab, half), integrals.dtype),
        scratch_shapes=[pltpu.SemaphoreType.DMA((held,))],
        compiler_params=pltpu.CompilerParams(vmem_limit_bytes=OWN_VMEM),
        name="own_half",
    )(integrals)


def pack_kernel(rows, slots, held, width, scalar_ref, x_ref, other_ref, mine_ref, table_ref, pick_ref):
    half = mine_ref.shape[1]
    core = scalar_ref[1]
    groups, picked, per_group = pick_ref.shape
    group = per_group // slots
    lane = lax.broadcasted_iota(jnp.int32, (1, per_group), 1)
    slot_lane, row_lane = lane % slots, lane // slots
    counts = [jnp.int32(0), jnp.int32(0)]
    lane_rank = jnp.zeros_like(lane)
    lane_irrep = jnp.zeros_like(lane)
    begin = jnp.where(scalar_ref[0] < 2, slots - held, 0) + held // 2
    for q in range(slots):
        position = lax.rem(begin + q, slots)
        slot = scalar_ref[2 + slots + position]
        irrep = scalar_ref[2 + slot]
        odd = irrep == 1
        rank = jnp.where(odd, counts[1], counts[0])
        counts = [jnp.where(odd, counts[0], counts[0] + 1), jnp.where(odd, counts[1] + 1, counts[1])]
        table_ref[position] = rank
        table_ref[slots + position] = irrep
        here = slot_lane == slot
        lane_rank = jnp.where(here, rank, lane_rank)
        lane_irrep = jnp.where(here, irrep, lane_irrep)
    table_ref[2 * slots] = scalar_ref[0]
    row = lax.broadcasted_iota(jnp.int32, (picked, per_group), 0)
    for g in range(groups):
        row_irrep = jnp.zeros_like(lane)
        for o in range(group):
            row_irrep = jnp.where(row_lane == o, scalar_ref[2 + 2 * slots + g * group + o], row_irrep)
        target = jnp.where(lane_irrep == row_irrep, lane_rank * group + row_lane, -1)
        pick_ref[g] = jnp.where(row == target, 1.0, 0.0).astype(pick_ref.dtype)

    for i in range(2 * half // width):
        into = mine_ref if i < half // width else other_ref
        at = i % (half // width) * width
        start = pl.multiple_of((core if i < half // width else 1 - core) * half + at, width)
        for g in range(groups):
            source = x_ref[g * per_group : (g + 1) * per_group, pl.ds(start, width)]
            packed = jnp.dot(pick_ref[g], source, preferred_element_type=jnp.float32).astype(x_ref.dtype)
            for j in range(picked // group):
                to = j * rows + g * group
                into[to : to + group, at : at + width] = packed[j * group : (j + 1) * group]


def pack(scalars, amplitudes, held):
    rows, slots, tile = amplitudes.shape
    live, half = slots // 2, tile // 2
    packed = jax.ShapeDtypeStruct((live * rows, half), amplitudes.dtype)
    vmem = pl.BlockSpec(memory_space=pltpu.VMEM)
    smem = pl.BlockSpec(memory_space=pltpu.SMEM)
    return pl.pallas_call(
        functools.partial(pack_kernel, rows, slots, held, half // 4),
        in_specs=[smem, vmem],
        out_specs=[vmem, vmem, smem],
        out_shape=[packed, packed, jax.ShapeDtypeStruct((2 * slots + 1,), jnp.int32)],
        scratch_shapes=[pltpu.VMEM((rows // 16, live * 16, 16 * slots), amplitudes.dtype)],
        compiler_params=pltpu.CompilerParams(vmem_limit_bytes=VMEM_LIMIT),
        cost_estimate=pl.CostEstimate(flops=0, bytes_accessed=3 * amplitudes.size, transcendentals=0),
        name="pack",
    )(scalars, amplitudes.reshape(rows * slots, tile))


def sum_kernel(rows, slots, tiles, work, table, ends, extra, scalar_ref, *refs):
    arrays, refs = refs[: tiles[-1][0] + 1], refs[tiles[-1][0] + 1 :]
    chunks, refs = refs[: len(table)], refs[len(table) :]
    total_ref = refs[-1]
    total_ref[...] = refs[0][...] if extra else jnp.zeros_like(total_ref)
    place = scalar_ref[2 * slots]
    for (low, high), used in work:
        for c in used:
            for i in range(chunks[c].shape[0]):
                position = jnp.int32(table[c][0][i])
                for z in range(1, len(table[c])):
                    position = jnp.where(place == z, table[c][z][i], position)

                @pl.when(position >= 0)
                def _():
                    at = jnp.maximum(position, 0)
                    start = scalar_ref[at] * rows
                    here = jnp.concatenate(
                        [arrays[t][pl.ds(pl.multiple_of(start + base, rows), rows), :] for t, base in tiles[low:high]], axis=0
                    )
                    term = lax.dot_general(here, chunks[c][i], NT, preferred_element_type=jnp.float32)
                    total_ref[scalar_ref[slots + at], low * rows : high * rows] += term

    if ends:
        blocks = refs[-1 - ends : -1]
        for t, out_ref in enumerate(blocks):
            size = total_ref.shape[1] // ends
            at = slice(t * size, (t + 1) * size)
            out = jnp.concatenate([total_ref[0, at], total_ref[1, at]], axis=1)
            if extra > 1 and (t + 1) * size <= refs[1].shape[0]:
                out = out + refs[1][at]
            out_ref[...] = out


def add_positions(scalars, arrays, tiles, rows, blocks, chunks, table, work, extra=(), ends=0, name="sum"):
    slots = scalars.shape[0] // 2
    ab = chunks[0].shape[1]
    vmem = pl.BlockSpec(memory_space=pltpu.VMEM)
    smem = pl.BlockSpec(memory_space=pltpu.SMEM)
    total = (2, blocks * rows, ab)
    end = jax.ShapeDtypeStruct((blocks * rows // max(ends, 1), 2 * ab), jnp.float32)
    return pl.pallas_call(
        functools.partial(sum_kernel, rows, slots, tuple(tiles), work, table, ends, len(extra)),
        in_specs=[smem] + [vmem] * (len(arrays) + len(chunks) + len(extra)),
        out_specs=[vmem] * ends if ends else vmem,
        out_shape=[end] * ends if ends else jax.ShapeDtypeStruct(total, jnp.float32),
        scratch_shapes=[pltpu.VMEM(total, jnp.float32)] if ends else [],
        compiler_params=pltpu.CompilerParams(vmem_limit_bytes=VMEM_LIMIT),
        cost_estimate=pl.CostEstimate(flops=0, bytes_accessed=1 << 22, transcendentals=0),
        name=name,
    )(scalars, *arrays, *chunks, *extra)


def after(array, *earlier):
    return lax.optimization_barrier((array, *earlier))[0] if earlier else array


def on_line(amplitudes, integrals, pair_irrep, slot_irrep, owner_slot_map):
    rows, slots, tile = amplitudes.shape
    place, side, core = lax.axis_index("pair"), lax.axis_index("ints"), lax.axis_index("rep")
    scalars = jnp.concatenate([jnp.stack([place, core]).astype(jnp.int32), slot_irrep, owner_slot_map, pair_irrep])
    across = [(i, 3 - i) for i in range(4)]
    beside = [(i, i ^ 2) for i in range(4)]

    own = own_half(integrals, tile)
    other, mine, scalars = pack(after(scalars, own), amplitudes, integrals.shape[1] // tile)
    held = slots // 4
    per = held // 2

    def held_at(places, low=0, high=held):
        return tuple((-1,) * (high - low) if z is None else tuple(range(z * held + low, z * held + high)) for z in places)

    home, near = (0, 1, 2, 3), (1, 0, 3, 2)
    middle, beyond = (None, 2, 1, None), (None, 3, 0, None)
    outer, outermost = (2, None, None, 1), (3, None, None, 0)
    chunks = {"own": (own, held_at(home))}
    tiles = [mine, lax.ppermute(other, "rep", SWAP)]

    def add(name, *step, arrays=None, at=None, blocks=4, extra=(), ends=0):
        names = []
        for *_, used in step:
            names += [n for n in used if n not in names]
        if arrays is None:
            arrays = tiles[: max(high for _, high, _ in step)]
            at = [(t, 0) for t in range(len(arrays))]
        return add_positions(
            scalars,
            arrays,
            at,
            rows,
            blocks,
            tuple(chunks[n][0] for n in names),
            tuple(chunks[n][1] for n in names),
            tuple(((low, high), tuple(names.index(n) for n in used)) for low, high, used in step),
            extra=extra,
            ends=ends,
            name=name,
        )

    def send(name, array, pairs, positions, *earlier):
        chunks[name] = (lax.ppermute(after(array, *earlier), "pair", pairs), positions)
        return chunks[name][0]

    low = per * rows
    near_chunk = send("near", own, NEAR, held_at(near))
    mid_chunk = send("mid", own, MIDDLE, held_at(middle))
    tiles.append(lax.ppermute(mine, ("ints", "rep"), beside))
    tiles.append(lax.ppermute(other, ("ints", "rep"), across))
    mid3_chunk = send("mid3", near_chunk[:per], MIDDLE, held_at(beyond, 0, per))
    send("out", mid_chunk, OUTWARD, held_at(outer))
    send("mid4", near_chunk[per:], MIDDLE, held_at(beyond, per))
    first = ("own", "mid", "near")
    sums = add("sum_near", (0, 1, first))
    sums = add("sum_side", (1, 3, first), extra=(sums,))
    heads = jnp.concatenate([t[:low] for t in tiles[:3]])
    heads = lax.ppermute(after(heads, sums), "pair", INWARD)
    send("out3", mid3_chunk, OUTWARD, held_at(outermost, 0, per), sums)
    last_heads = lax.ppermute(tiles[3][:low], "pair", INWARD)
    rows_at = [(0, t * low) for t in range(3)]
    away = add("sum_away", (0, 3, ("mid4",)), arrays=[after(heads, sums)], at=rows_at, blocks=3, ends=1)
    back = lax.ppermute(away[0], "pair", OUTWARD)
    sums = add("sum_most", (3, 4, first), (0, 4, ("mid3", "mid4", "out")), extra=(after(sums, away[0]),))
    away = add("sum_last_away", (0, 1, ("mid4",)), arrays=[after(last_heads, sums)], at=[(0, 0)], blocks=1, ends=1)
    home_pairs = [(4 * a + i, 4 * b + 3 - i) for a, b in OUTWARD for i in range(4)]
    back_across = lax.ppermute(away[0], ("pair", "ints", "rep"), home_pairs)
    sums = add("sum_last", (0, 4, ("out3",)), extra=(after(sums, away[0]), back), ends=4)

    own = sums[0] + lax.ppermute(sums[1], "rep", SWAP)
    theirs = lax.ppermute(sums[2], ("ints", "rep"), beside) + lax.ppermute(sums[3], ("ints", "rep"), across)
    theirs = theirs + back_across
    ab = integrals.shape[0]
    odd = (pair_irrep == 1)[:, None]
    own = jnp.where(odd, own[:, ab:], own[:, :ab])
    theirs = jnp.where(odd, theirs[:, ab:], theirs[:, :ab])
    return jnp.where(side == 0, jnp.concatenate([own, theirs], axis=1), jnp.concatenate([theirs, own], axis=1))


def solution(mesh):
    placed = (
        P(("groups", "pair", "ints", "rep"), None, None),
        P(("groups", "ints"), "pair"),
        P(("groups", "pair", "ints", "rep")),
        P("groups"),
        P("groups"),
    )
    line = mesh.shape["pair"] == 4 and mesh.shape["ints"] == 2 and mesh.shape["rep"] == 2
    return jax.shard_map(
        on_line if line else plain,
        mesh=mesh,
        in_specs=placed,
        out_specs=P(("groups", "pair", "ints", "rep"), None),
        check_vma=False,
    )
```
